512 devices in a mesh: dp: 32 (over y_hi, z), expert: 16 (over x, y_lo, core).
Axes of the slice: x: 4, y: 4 (y_hi: 2, y_lo: 2; y = y_hi * 2 + y_lo), z: 16, core: 2. Of those that a mesh axis runs over, the one named last changes fastest.
Arguments:
- images: bfloat16 [1536, 128, 640], P(('dp', 'expert')), may hold values from -24 to 24
- router: bfloat16 [640, 128], replicated, as said below
- w_in: bfloat16 [16, 640, 2560], P('expert', 'dp'), may hold values from -18 to 18, as said below
- w_out: bfloat16 [16, 2560, 640], P('expert', 'dp'), may hold values from -18 to 18, as said below
- history: float32 [16, 2, 16], P('expert'), may hold values from 2 to 8
- cotangent: bfloat16 [1536, 128, 640], P(('dp', 'expert')), may hold values from -6 to 6
Outputs:
- output: bfloat16 [1536, 128, 640], P(('dp', 'expert'))
- d_images: bfloat16 [1536, 128, 640], P(('dp', 'expert'))
- d_w_in: bfloat16 [16, 640, 2560], P('expert', 'dp')
- new_history: float32 [16, 2, 16], P('expert')
The draws below stay inside these ranges and needn't reach their ends.
Inputs may be any that keep to these rules, and one draw needn't show every extreme that they name: `w_in`: of order one in the first of the 640 rows, growing linearly along the rows to several times that; scaled by scale_in. `w_out`: of order one in the first of the 2560 rows, growing linearly along the rows to several times that; scaled by scale_out. `router`: of order one over the square root of 640, or larger.
All inputs are finite; a program needn't handle non-finite values.
Results may differ from the reference program's by a relative error of at most 0.025.
Values may be sent and summed in bfloat16 or wider, within the bound.
No kernel may reach another device: no remote copies, remote signals or barrier semaphores. Data moves between devices by JAX's collectives and lax.ppermute only.
A program may use at most 64 MiB of HBM per device.

```python
import math
import jax
import jax.numpy as jnp
from jax import lax

MODEL_WIDTH = 640
FF = 2560
PATCH = 128
SLOTS = 8
HIST = 16
EXPERTS = 16
IMAGE_SLOTS = 128
IMAGES = 1536
N_DP = 32


def ramped(key, shape, top):
    base = jax.random.truncated_normal(key, -6.0, 6.0, shape, jnp.float32)
    steps = jnp.arange(shape[1], dtype=jnp.float32) / max(shape[1] - 1, 1)
    return base * (1.0 + (top - 1.0) * steps)[None, :, None]


def draw_w_in(key, part):
    key = jax.random.fold_in(key, 11)
    top = 3.0
    return ramped(key, (EXPERTS, MODEL_WIDTH, FF), top).astype(jnp.bfloat16)


def draw_w_out(key, part):
    key = jax.random.fold_in(key, 23)
    top = 3.0
    return ramped(key, (EXPERTS, FF, MODEL_WIDTH), top).astype(jnp.bfloat16)


def draw_router(key, part):
    key = jax.random.fold_in(key, 37)
    first_operand = jax.random.fold_in(key, 0)
    value_entries = jax.random.truncated_normal(first_operand, -6.0, 6.0, (MODEL_WIDTH, IMAGE_SLOTS), jnp.float32) * 1.5
    return (value_entries / jnp.sqrt(jnp.float32(MODEL_WIDTH))).astype(jnp.bfloat16)


def raised(entries, key, source, target, blocks, factor):
    owner, partner = [(jnp.arange(entries.shape[position]) // (entries.shape[position] // blocks)).reshape([-1 if axis == position else 1 for axis in range(entries.ndim)]) for position in (source, target)]
    chosen = jax.random.permutation(key, blocks)[partner]
    strong = (owner == chosen) | (owner == (partner + blocks // 2) % blocks)
    return jnp.where(strong, factor * entries, entries)


def steps_of(rng, dims, cuts, low, largest):
    gain, own = 1.0, jax.random.fold_in(rng, 6)
    for axis_at, shards_of in cuts:
        draws = jnp.exp(jax.random.uniform(jax.random.fold_in(own, axis_at), (shards_of,), jnp.float32, low / len(cuts), largest / len(cuts)))
        gain = gain * jnp.repeat(draws, dims[axis_at] // shards_of).reshape([-1 if axis == axis_at else 1 for axis in range(len(dims))])
    return gain


def noise(rng, shape, deviation, most, cuts=(), held_as=jnp.bfloat16):
    array = deviation * jax.random.normal(rng, shape, jnp.float32)
    if cuts:
        array = array * steps_of(rng, shape, cuts, -0.22, 0.18)
    return jnp.clip(array, -most, most).astype(held_as)


def gaussian_with(rng, extent, scale, most, cuts, heavy, held_as=jnp.bfloat16):
    entries = scale * jax.random.normal(rng, extent, jnp.float32)
    if cuts:
        entries = entries * steps_of(rng, extent, cuts, -0.22, 0.18)
    return jnp.clip(raised(entries, jax.random.fold_in(rng, 3), *heavy), -most, most).astype(held_as)


def setup_inputs(seed: int = 0) -> dict:
    seeds = jax.random.split(jax.random.key(seed), 7)
    return {
        "images": gaussian_with(seeds[0], (IMAGES, PATCH, MODEL_WIDTH), 1.0, 24.0, ((0, 512),), (0, 2, 128, 5.5)),
        "router": draw_router(jax.random.fold_in(seeds[6], 71), 0),
        "w_in": draw_w_in(jax.random.fold_in(seeds[6], 71), 0),
        "w_out": draw_w_out(jax.random.fold_in(seeds[6], 71), 0),
        "history": jnp.clip(jnp.exp(math.log(8.0) - 1.3862944 * jax.random.uniform(seeds[4], (EXPERTS, 2, HIST), jnp.float32) ** steps_of(seeds[4], (EXPERTS, 2, HIST), ((0, 16),), -0.2, 0.2)), 2.0, 8.0),
        "cotangent": noise(seeds[5], (IMAGES, PATCH, MODEL_WIDTH), 1.0, 6.0, ((0, 512),)),
    }


def gelu_back(pre_act, d_hidden):
    _, pullback = jax.vjp(jax.nn.gelu, pre_act)
    return pullback(d_hidden)[0]

def to_experts(slot_rows):
    count = slot_rows.shape[0]
    width = slot_rows.shape[-1]
    shaped = slot_rows.reshape(count, EXPERTS, SLOTS, width)
    return jnp.transpose(shaped, (1, 0, 2, 3)).reshape(EXPERTS, count * SLOTS, width)

def from_experts(expert_rows):
    width = expert_rows.shape[-1]
    shaped = expert_rows.reshape(EXPERTS, -1, SLOTS, width)
    return jnp.transpose(shaped, (1, 0, 2, 3)).reshape(-1, EXPERTS * SLOTS, width)

def reference(images, router, w_in, w_out, history, cotangent):
    logits = jnp.einsum('bpd,ds->bps', images.astype(jnp.float32), router.astype(jnp.float32))
    dispatch = jax.nn.softmax(logits, axis=1)
    combine = jax.nn.softmax(logits, axis=2)
    dispatch_batch = dispatch.astype(jnp.bfloat16)
    combine_b = combine.astype(jnp.bfloat16)
    slot_in = jnp.einsum('bps,bpd->bsd', dispatch_batch.astype(jnp.float32), images.astype(jnp.float32)).astype(jnp.bfloat16)
    scale_in = lax.optimization_barrier(jnp.max(history[:, 0, :], axis=-1)) / 448.0
    scale_out = lax.optimization_barrier(jnp.max(history[:, 1, :], axis=-1)) / 448.0
    rows_all = to_experts(slot_in)

    def forward_one(packed):
        rows, weight_in, weight_out, s_in, s_out = packed
        pre_act = jnp.dot(rows, weight_in, preferred_element_type=jnp.float32) * s_in
        hidden = jax.nn.gelu(pre_act).astype(jnp.bfloat16)
        return (jnp.dot(hidden, weight_out, preferred_element_type=jnp.float32) * s_out).astype(jnp.bfloat16)
    outs_all = lax.map(forward_one, (rows_all, w_in, w_out, scale_in, scale_out))
    slot_out = from_experts(outs_all)
    output = jnp.einsum('bps,bsd->bpd', combine_b.astype(jnp.float32), slot_out.astype(jnp.float32)).astype(jnp.bfloat16)
    d_combine = jnp.einsum('bpd,bsd->bps', cotangent.astype(jnp.float32), slot_out.astype(jnp.float32))
    d_slot_out = jnp.einsum('bps,bpd->bsd', combine_b.astype(jnp.float32), cotangent.astype(jnp.float32)).astype(jnp.bfloat16)
    grads_all = to_experts(d_slot_out)
    groups = N_DP

    def backward_one(packed):
        rows, d_rows, weight_in, weight_out, s_in, s_out = packed
        pre_act = jnp.dot(rows, weight_in, preferred_element_type=jnp.float32) * s_in
        d_hidden = jnp.dot(d_rows, weight_out.T, preferred_element_type=jnp.float32) * s_out
        d_pre = gelu_back(pre_act, d_hidden).astype(jnp.bfloat16)
        rows_g = rows.reshape(groups, -1, rows.shape[-1]).astype(jnp.float32)
        pre_g = d_pre.reshape(groups, -1, d_pre.shape[-1]).astype(jnp.float32)
        terms = jnp.einsum('kgd,kgf->kdf', rows_g, pre_g) * s_in
        d_weight = lax.optimization_barrier(jnp.sum(terms.astype(jnp.bfloat16).astype(jnp.float32), axis=0)).astype(jnp.bfloat16)
        d_rows_in = (jnp.dot(d_pre, weight_in.T, preferred_element_type=jnp.float32) * s_in).astype(jnp.bfloat16)
        return (d_weight, d_rows_in)
    d_w_in, d_in_all = lax.map(backward_one, (rows_all, grads_all, w_in, w_out, scale_in, scale_out))
    d_slot_in = from_experts(d_in_all)
    d_dispatch = jnp.einsum('bpd,bsd->bps', images.astype(jnp.float32), d_slot_in.astype(jnp.float32))
    d_logits = dispatch * (d_dispatch - lax.optimization_barrier(jnp.sum(dispatch * d_dispatch, axis=1, keepdims=True)))
    d_logits = d_logits + combine * (d_combine - lax.optimization_barrier(jnp.sum(combine * d_combine, axis=2, keepdims=True)))
    d_logits = d_logits.astype(jnp.bfloat16)
    d_images = jnp.einsum('bps,bsd->bpd', dispatch_batch.astype(jnp.float32), d_slot_in.astype(jnp.float32))
    d_images = d_images + jnp.einsum('bps,ds->bpd', d_logits.astype(jnp.float32), router.astype(jnp.float32))
    d_images = d_images.astype(jnp.bfloat16)
    peak_in = lax.optimization_barrier(jnp.max(jnp.abs(w_in.astype(jnp.float32)), axis=(1, 2)))
    peak_out = lax.optimization_barrier(jnp.max(jnp.abs(w_out.astype(jnp.float32)), axis=(1, 2)))
    peaks = jnp.stack([peak_in, peak_out], axis=1)
    new_history = jnp.concatenate([peaks[:, :, None], history[:, :, :-1]], axis=2)
    return (output, d_images, d_w_in, new_history)
```

```python
import jax
import jax.numpy as jnp
import numpy as np
from jax import lax
from jax.experimental import pallas as pl
from jax.experimental.pallas import tpu as pltpu
from jax.sharding import Mesh
from jax.sharding import PartitionSpec as P

PAD = 48
CHUNK = 640
C0 = 0.7978845608028654
C1 = 0.044715


def expert_kernel(scale_ref, rows_ref, grad_ref, w_in_ref, w_out_ref, dw_ref, out_ref, drow_ref, out_acc, drow_acc):
    step = pl.program_id(0)
    scale_in = scale_ref[0]
    scale_out = scale_ref[1]
    rows = rows_ref[...]
    grad = grad_ref[...]
    w_in = w_in_ref[...].reshape(rows.shape[1], -1)
    w_out = w_out_ref[...].reshape(-1, grad.shape[1])
    pre = jnp.dot(rows, w_in, preferred_element_type=jnp.float32) * scale_in
    d_hidden = (
        lax.dot_general(grad, w_out, (((1,), (1,)), ((), ())), preferred_element_type=jnp.float32)
        * scale_out
    )
    square = pre * pre
    tanh = jnp.tanh(C0 * (pre + C1 * (square * pre)))
    half = 0.5 * (1.0 + tanh)
    hidden = (pre * half).astype(jnp.bfloat16)
    slope = half + (0.5 * C0) * pre * (1.0 - tanh * tanh) * (1.0 + (3.0 * C1) * square)
    d_pre = (slope * d_hidden).astype(jnp.bfloat16)
    dw = lax.dot_general(rows, d_pre, (((0,), (0,)), ((), ())), preferred_element_type=jnp.float32)
    dw_ref[...] = (dw * scale_in).astype(dw_ref.dtype)
    out = jnp.dot(hidden, w_out, preferred_element_type=jnp.float32)
    drow = lax.dot_general(d_pre, w_in, (((1,), (1,)), ((), ())), preferred_element_type=jnp.float32)

    @pl.when(step == 0)
    def _():
        out_acc[...] = out
        drow_acc[...] = drow

    @pl.when(step > 0)
    def _():
        out_acc[...] += out
        drow_acc[...] += drow

    @pl.when(step == pl.num_programs(0) - 1)
    def _():
        out_ref[...] = (out_acc[...] * scale_out).astype(out_ref.dtype)
        drow_ref[...] = (drow_acc[...] * scale_in).astype(drow_ref.dtype)


def experts(scales, rows, grads, weights):
    count, depth = rows.shape
    width = grads.shape[1]
    zs = weights.shape[0]
    chunks = 4
    return pl.pallas_call(
        expert_kernel,
        grid=(chunks,),
        in_specs=[
            pl.BlockSpec(memory_space=pltpu.SMEM),
            pl.BlockSpec((count, depth), lambda r: (0, 0)),
            pl.BlockSpec((count, width), lambda r: (0, 0)),
            pl.BlockSpec((zs, PAD, CHUNK), lambda r: (0, 4 + r, 0)),
            pl.BlockSpec((zs // 2, 80, width), lambda r: (r % 2, r // 2, 0)),
        ],
        out_specs=[
            pl.BlockSpec((depth, CHUNK), lambda r: (0, r)),
            pl.BlockSpec((count, width), lambda r: (0, 0)),
            pl.BlockSpec((count, depth), lambda r: (0, 0)),
        ],
        out_shape=[
            jax.ShapeDtypeStruct((depth, chunks * CHUNK), jnp.bfloat16),
            jax.ShapeDtypeStruct((count, width), jnp.bfloat16),
            jax.ShapeDtypeStruct((count, depth), jnp.bfloat16),
        ],
        scratch_shapes=[
            pltpu.VMEM((count, width), jnp.float32),
            pltpu.VMEM((count, depth), jnp.float32),
        ],
        compiler_params=pltpu.CompilerParams(vmem_limit_bytes=40 * 1024 * 1024),
        cost_estimate=pl.CostEstimate(
            flops=10 * count * width * chunks * CHUNK,
            bytes_accessed=16 * 1024 * 1024,
            transcendentals=count * chunks * CHUNK,
        ),
    )(scales, rows, grads, weights, weights)


def placement(width, zs):
    per = width // (2 * zs)
    table = np.zeros((width, zs * PAD), np.float32)
    for half in range(2):
        for z in range(zs):
            for i in range(per):
                table[(half * zs + z) * per + i, z * PAD + half * per + i] = 1.0
    return table


def body(images, router, w_in, w_out, history, cotangent):
    bf16 = jnp.bfloat16
    f32 = jnp.float32
    width = images.shape[2]
    count = images.shape[0]
    zs = lax.axis_size("z")
    n_expert = lax.axis_size("x") * lax.axis_size("yl") * lax.axis_size("c")
    per_expert = router.shape[1] // n_expert
    along = ("x", "yl", "c")
    half = lax.axis_index("yh")

    local_out = w_out[0]
    local_in = w_in[0]
    mine = jnp.concatenate([local_in.reshape(20, 4, CHUNK).transpose(1, 0, 2).reshape(80, CHUNK), local_out], 0)
    other = lax.ppermute(mine, "yh", [(0, 1), (1, 0)])
    low = jnp.where(half == 0, mine, other)
    high = jnp.where(half == 0, other, mine)
    gap = jnp.zeros((4, PAD - 40, CHUNK), bf16)
    in_part = jnp.concatenate(
        [low[:80].reshape(4, 20, CHUNK), high[:80].reshape(4, 20, CHUNK), gap], 1
    ).reshape(4 * PAD, CHUNK)
    out_part = jnp.concatenate([low[80:], high[80:]], 0)
    peak_in = jnp.full((16, CHUNK), jnp.max(jnp.abs(in_part)))
    peak_out = jnp.full((16, CHUNK), jnp.max(jnp.abs(out_part)))
    block = jnp.concatenate([out_part, peak_in, peak_out, in_part], 0)
    weights = lax.all_gather(block, "z", axis=0, tiled=False)

    logits = jnp.einsum("bpd,ds->bps", images, router, preferred_element_type=f32)
    dispatch = jax.nn.softmax(logits, axis=1)
    combine = jax.nn.softmax(logits, axis=2)
    dispatch_b = dispatch.astype(bf16)
    combine_b = combine.astype(bf16)
    slot_in = jnp.einsum("bps,bpd->bsd", dispatch_b, images, preferred_element_type=f32).astype(bf16)
    d_slot_out = jnp.einsum("bps,bpd->bsd", combine_b, cotangent, preferred_element_type=f32).astype(bf16)
    both = jnp.stack([slot_in, d_slot_out]).reshape(2, count, n_expert, per_expert, width)
    both = both.transpose(2, 0, 1, 3, 4)
    routed = lax.all_to_all(both, along, split_axis=0, concat_axis=0, tiled=True)
    rows = routed[:, 0].reshape(-1, width)
    grads = routed[:, 1].reshape(-1, width)
    spread = jnp.asarray(placement(width, zs), bf16)
    rows = jnp.dot(rows, spread, preferred_element_type=f32).astype(bf16)

    scales = jnp.max(history[0], axis=1) / 448.0
    dw, rows_out, d_rows = experts(scales, rows, grads, weights)
    d_rows = lax.dot_general(
        d_rows, spread, (((1,), (1,)), ((), ())), preferred_element_type=f32
    ).astype(bf16)

    part = lax.psum_scatter(dw, "z", scatter_dimension=0, tiled=True)
    keep = jnp.where(half == 0, part[:20], part[20:40])
    send = jnp.where(half == 0, part[20:40], part[:20])
    got = lax.ppermute(send, "yh", [(0, 1), (1, 0)])
    d_w_in = (keep.astype(f32) + got.astype(f32)).astype(bf16)[None]

    back = jnp.stack(
        [rows_out.reshape(n_expert, -1, width), d_rows.reshape(n_expert, -1, width)], 1
    ).reshape(n_expert, 2, count, per_expert, width)
    returned = lax.all_to_all(back, along, split_axis=0, concat_axis=0, tiled=True)
    returned = returned.transpose(1, 2, 0, 3, 4).reshape(2, count, -1, width)
    slot_out = returned[0]
    d_slot_in = returned[1]
    output = jnp.einsum("bps,bsd->bpd", combine_b, slot_out, preferred_element_type=f32).astype(bf16)
    d_combine = jnp.einsum("bpd,bsd->bps", cotangent, slot_out, preferred_element_type=f32)
    d_dispatch = jnp.einsum("bpd,bsd->bps", images, d_slot_in, preferred_element_type=f32)
    d_logits = dispatch * (d_dispatch - jnp.sum(dispatch * d_dispatch, axis=1, keepdims=True))
    d_logits = d_logits + combine * (d_combine - jnp.sum(combine * d_combine, axis=2, keepdims=True))
    d_logits = d_logits.astype(bf16)
    d_images = jnp.einsum("bps,bsd->bpd", dispatch_b, d_slot_in, preferred_element_type=f32)
    d_images = d_images + jnp.einsum("bps,ds->bpd", d_logits, router, preferred_element_type=f32)
    d_images = d_images.astype(bf16)

    peaks = jnp.max(weights[:, 160:192:16, 0], axis=0).astype(f32)
    new_history = jnp.concatenate([peaks[:, None], history[0, :, :-1]], axis=1)[None]
    return (output, d_images, d_w_in, new_history)


def solution(mesh):
    fine = Mesh(mesh.devices.reshape(2, 16, 4, 2, 2), ("yh", "z", "x", "yl", "c"))
    dp = ("yh", "z")
    expert = ("x", "yl", "c")
    every = dp + expert
    return jax.shard_map(
        body,
        mesh=fine,
        in_specs=(
            P(every, None, None),
            P(),
            P(expert, dp, None),
            P(expert, dp, None),
            P(expert, None, None),
            P(every, None, None),
        ),
        out_specs=(
            P(every, None, None),
            P(every, None, None),
            P(expert, dp, None),
            P(expert, None, None),
        ),
        check_vma=False,
    )
```

```python
import jax
import jax.numpy as jnp
import numpy as np
from jax import lax
from jax.experimental import pallas as pl
from jax.experimental.pallas import tpu as pltpu
from jax.sharding import Mesh
from jax.sharding import PartitionSpec as P

PAD = 48
CHUNK = 640
STRIDE = 64
SWAP = ((0, 1), (1, 0))
C0 = 0.7978845608028654
C1 = 0.044715


def hidden_kernel(scale_ref, rows_ref, grad_ref, w_in_ref, w_out_ref, dw_ref, hidden_ref, dpre_ref):
    scale_in = scale_ref[0]
    scale_out = scale_ref[1]
    rows = rows_ref[...]
    grad = grad_ref[...]
    w_in = w_in_ref[...].reshape(rows.shape[1], -1)
    w_out = w_out_ref[...].reshape(-1, grad.shape[1])
    pre = jnp.dot(rows, w_in, preferred_element_type=jnp.float32) * scale_in
    d_hidden = (
        lax.dot_general(grad, w_out, (((1,), (1,)), ((), ())), preferred_element_type=jnp.float32)
        * scale_out
    )
    square = pre * pre
    tanh = jnp.tanh(C0 * (pre + C1 * (square * pre)))
    half = 0.5 * (1.0 + tanh)
    hidden_ref[...] = (pre * half).astype(jnp.bfloat16)
    slope = half + (0.5 * C0) * pre * (1.0 - tanh * tanh) * (1.0 + (3.0 * C1) * square)
    d_pre = (slope * d_hidden).astype(jnp.bfloat16)
    dpre_ref[...] = d_pre
    dw = lax.dot_general(rows, d_pre, (((0,), (0,)), ((), ())), preferred_element_type=jnp.float32)
    dw = (dw * scale_in).astype(dw_ref.dtype)
    for z in range(dw.shape[0] // PAD):
        dw_ref[z * STRIDE : z * STRIDE + PAD] = dw[z * PAD : (z + 1) * PAD]
        dw_ref[z * STRIDE + PAD : (z + 1) * STRIDE] = jnp.zeros((STRIDE - PAD, CHUNK), dw_ref.dtype)


def hidden_of(scales, rows, grads, weights):
    count, depth = rows.shape
    width = grads.shape[1]
    zs = weights.shape[0]
    chunks = 2
    by_chunk = pl.BlockSpec((count, CHUNK), lambda r: (0, r))
    return pl.pallas_call(
        hidden_kernel,
        grid=(chunks,),
        in_specs=[
            pl.BlockSpec(memory_space=pltpu.SMEM),
            pl.BlockSpec((count, depth), lambda r: (0, 0)),
            pl.BlockSpec((count, width), lambda r: (0, 0)),
            pl.BlockSpec((zs, PAD, CHUNK), lambda r: (0, 2 + r, 0)),
            pl.BlockSpec((zs // 2, 80, width), lambda r: (r, 0, 0)),
        ],
        out_specs=[pl.BlockSpec((zs * STRIDE, CHUNK), lambda r: (0, r)), by_chunk, by_chunk],
        out_shape=[
            jax.ShapeDtypeStruct((zs * STRIDE, chunks * CHUNK), jnp.bfloat16),
            jax.ShapeDtypeStruct((count, chunks * CHUNK), jnp.bfloat16),
            jax.ShapeDtypeStruct((count, chunks * CHUNK), jnp.bfloat16),
        ],
        compiler_params=pltpu.CompilerParams(vmem_limit_bytes=40 * 1024 * 1024),
        cost_estimate=pl.CostEstimate(
            flops=6 * count * width * chunks * CHUNK,
            bytes_accessed=16 * 1024 * 1024,
            transcendentals=count * chunks * CHUNK,
        ),
    )(scales, rows, grads, weights, weights)


def rows_kernel(
    scale_ref, hidden_ref, dpre_ref, w_in_ref, w_out_ref,
    out_own_ref, drow_own_ref, out_sent_ref, drow_sent_ref, peak_ref, out_acc, drow_acc,
):
    step = pl.program_id(0)
    scale_in = scale_ref[0]
    scale_out = scale_ref[1]
    w_in = w_in_ref[...].reshape(drow_acc.shape[1], -1)
    w_out = w_out_ref[...].reshape(-1, out_acc.shape[1])
    out = jnp.dot(hidden_ref[...], w_out, preferred_element_type=jnp.float32)
    drow = lax.dot_general(
        dpre_ref[...], w_in, (((1,), (1,)), ((), ())), preferred_element_type=jnp.float32
    )
    peak_in = jnp.max(jnp.abs(w_in.astype(jnp.float32)), axis=0, keepdims=True)
    peak_out = jnp.max(jnp.abs(w_out.astype(jnp.float32)), axis=0, keepdims=True)

    @pl.when(step == 0)
    def _():
        out_acc[...] = out
        drow_acc[...] = drow
        peak_ref[:, :CHUNK] = jnp.broadcast_to(peak_in, (8, CHUNK))
        peak_ref[:, CHUNK:] = jnp.broadcast_to(peak_out, (8, CHUNK))

    @pl.when(step > 0)
    def _():
        count = out_own_ref.shape[0]
        width = out_own_ref.shape[1]
        out_sum = (out_acc[...] + out) * scale_out
        drow_sum = (drow_acc[...] + drow) * scale_in
        out_own_ref[...] = out_sum[:count]
        drow_own_ref[...] = drow_sum[:count]
        out_sent_ref[...] = out_sum[count:].astype(out_sent_ref.dtype)
        drow_sent_ref[...] = drow_sum[count:].astype(drow_sent_ref.dtype)
        peak_ref[:, :CHUNK] = jnp.maximum(peak_ref[:, :CHUNK], peak_in)
        peak_ref[:, CHUNK:] = jnp.maximum(peak_ref[:, CHUNK:], peak_out)


def rows_of(scales, hidden, dpre, weights, depth):
    count = hidden.shape[0]
    zs, _, width = weights.shape
    chunks = 2
    half = count // 2
    by_chunk = pl.BlockSpec((count, CHUNK), lambda r: (0, r))
    return pl.pallas_call(
        rows_kernel,
        grid=(chunks,),
        in_specs=[
            pl.BlockSpec(memory_space=pltpu.SMEM),
            by_chunk,
            by_chunk,
            pl.BlockSpec((zs, PAD, CHUNK), lambda r: (0, 2 + r, 0)),
            pl.BlockSpec((zs // 2, 80, width), lambda r: (r, 0, 0)),
        ],
        out_specs=[
            pl.BlockSpec((half, width), lambda r: (0, 0)),
            pl.BlockSpec((half, depth), lambda r: (0, 0)),
            pl.BlockSpec((half, width), lambda r: (0, 0)),
            pl.BlockSpec((half, depth), lambda r: (0, 0)),
            pl.BlockSpec((8, 2 * CHUNK), lambda r: (0, 0)),
        ],
        out_shape=[
            jax.ShapeDtypeStruct((half, width), jnp.float32),
            jax.ShapeDtypeStruct((half, depth), jnp.float32),
            jax.ShapeDtypeStruct((half, width), jnp.bfloat16),
            jax.ShapeDtypeStruct((half, depth), jnp.bfloat16),
            jax.ShapeDtypeStruct((8, 2 * CHUNK), jnp.float32),
        ],
        scratch_shapes=[
            pltpu.VMEM((count, width), jnp.float32),
            pltpu.VMEM((count, depth), jnp.float32),
        ],
        compiler_params=pltpu.CompilerParams(vmem_limit_bytes=40 * 1024 * 1024),
        cost_estimate=pl.CostEstimate(
            flops=4 * count * width * chunks * CHUNK,
            bytes_accessed=16 * 1024 * 1024,
            transcendentals=0,
        ),
    )(scales, hidden, dpre, weights, weights)


def placement(width, zs):
    per = width // (2 * zs)
    table = np.zeros((width, zs * PAD), np.float32)
    for half in range(2):
        for z in range(zs):
            for i in range(per):
                table[(half * zs + z) * per + i, z * PAD + half * per + i] = 1.0
    return table


def body(images, router, w_in, w_out, history, cotangent):
    bf16 = jnp.bfloat16
    f32 = jnp.float32
    width = images.shape[2]
    count = images.shape[0]
    zs = lax.axis_size("z")
    n_expert = lax.axis_size("x") * lax.axis_size("yl") * lax.axis_size("c")
    per_expert = router.shape[1] // n_expert
    along = ("x", "yl", "c")
    yh = lax.axis_index("yh")

    local = w_in[0]
    ff = local.shape[1] // 2
    stay = jnp.where(yh == 0, local[:, :ff], local[:, ff:])
    swap = jnp.where(yh == 0, local[:, ff:], local[:, :ff])
    got = lax.ppermute(swap, "yh", SWAP)
    stay = jnp.stack([stay[:, :CHUNK], stay[:, CHUNK:]])
    got = jnp.stack([got[:, :CHUNK], got[:, CHUNK:]])
    low = jnp.where(yh == 0, stay, got)
    high = jnp.where(yh == 0, got, stay)
    gap = jnp.zeros((2, PAD - 40, CHUNK), bf16)
    in_part = jnp.concatenate([low, high, gap], 1).reshape(2 * PAD, CHUNK)
    block = jnp.concatenate([w_out[0], jnp.zeros((16, CHUNK), bf16), in_part], 0)
    weights = lax.all_gather(block, "z", axis=0, tiled=False)

    scales = jnp.max(history[0], axis=1) / 448.0

    logits = jnp.einsum("bpd,ds->bps", images, router, preferred_element_type=f32)
    dispatch = jax.nn.softmax(logits, axis=1)
    combine = jax.nn.softmax(logits, axis=2)
    dispatch_b = dispatch.astype(bf16)
    combine_b = combine.astype(bf16)
    slot_in = jnp.einsum("bps,bpd->bsd", dispatch_b, images, preferred_element_type=f32).astype(bf16)
    d_slot_out = jnp.einsum("bps,bpd->bsd", combine_b, cotangent, preferred_element_type=f32).astype(bf16)
    both = jnp.stack([slot_in, d_slot_out]).reshape(2, count, n_expert, per_expert, width)
    both = both.transpose(2, 0, 1, 3, 4)
    routed = lax.all_to_all(both, along, split_axis=0, concat_axis=0, tiled=True)
    routed = routed.transpose(1, 0, 2, 3, 4).reshape(2, -1, width)
    twin = lax.ppermute(routed, "yh", SWAP)
    rows = jnp.concatenate([routed[0], twin[0]], 0)
    grads = jnp.concatenate([routed[1], twin[1]], 0)
    spread = jnp.asarray(placement(width, zs), bf16)
    rows = jnp.dot(rows, spread, preferred_element_type=f32).astype(bf16)

    dw, hidden, dpre = hidden_of(scales, rows, grads, weights)

    out_own, drow_own, out_sent, drow_sent, peaks = rows_of(scales, hidden, dpre, weights, rows.shape[1])
    fetched = lax.ppermute(jnp.concatenate([out_sent, drow_sent], 1), "yh", SWAP)
    rows_out = (out_own + fetched[:, :width].astype(f32)).astype(bf16)
    d_rows = (drow_own + fetched[:, width:].astype(f32)).astype(bf16)
    d_rows = lax.dot_general(
        d_rows, spread, (((1,), (1,)), ((), ())), preferred_element_type=f32
    ).astype(bf16)
    back = jnp.stack(
        [rows_out.reshape(n_expert, -1, width), d_rows.reshape(n_expert, -1, width)], 1
    ).reshape(n_expert, 2, count, per_expert, width)
    returned = lax.all_to_all(back, along, split_axis=0, concat_axis=0, tiled=True)
    returned = returned.transpose(1, 2, 0, 3, 4).reshape(2, count, -1, width)

    part = lax.psum_scatter(dw, "z", scatter_dimension=0, tiled=True)
    keep = jnp.where(yh == 0, part[:20], part[20:40])
    give = jnp.where(yh == 0, part[20:40], part[:20])
    peaks = peaks[:1].astype(bf16)
    got = lax.ppermute(jnp.concatenate([give, peaks], 0), "yh", SWAP)
    theirs = got[:20]
    d_w_in = jnp.concatenate(
        [jnp.where(yh == 0, keep, theirs), jnp.where(yh == 0, theirs, keep)], 1
    )[None]
    peaks = jnp.maximum(peaks[0], got[20]).reshape(2, -1).astype(f32)
    peaks = jnp.max(peaks, axis=1, keepdims=True)
    new_history = jnp.concatenate([peaks, history[0, :, :-1]], axis=1)[None]

    slot_out = returned[0]
    d_slot_in = returned[1]
    output = jnp.einsum("bps,bsd->bpd", combine_b, slot_out, preferred_element_type=f32).astype(bf16)
    d_combine = jnp.einsum("bpd,bsd->bps", cotangent, slot_out, preferred_element_type=f32)
    d_dispatch = jnp.einsum("bpd,bsd->bps", images, d_slot_in, preferred_element_type=f32)
    d_logits = dispatch * (d_dispatch - jnp.sum(dispatch * d_dispatch, axis=1, keepdims=True))
    d_logits = d_logits + combine * (d_combine - jnp.sum(combine * d_combine, axis=2, keepdims=True))
    d_logits = d_logits.astype(bf16)
    d_images = jnp.einsum("bps,bsd->bpd", dispatch_b, d_slot_in, preferred_element_type=f32)
    d_images = d_images + jnp.einsum("bps,ds->bpd", d_logits, router, preferred_element_type=f32)
    d_images = d_images.astype(bf16)
    return (output, d_images, d_w_in, new_history)


def solution(mesh):
    fine = Mesh(mesh.devices.reshape(2, 16, 4, 2, 2), ("yh", "z", "x", "yl", "c"))
    dp = ("yh", "z")
    expert = ("x", "yl", "c")
    every = dp + expert
    return jax.shard_map(
        body,
        mesh=fine,
        in_specs=(
            P(every, None, None),
            P(),
            P(expert, dp, None),
            P(expert, dp, None),
            P(expert, None, None),
            P(every, None, None),
        ),
        out_specs=(
            P(every, None, None),
            P(every, None, None),
            P(expert, dp, None),
            P(expert, None, None),
        ),
        check_vma=False,
    )
```

```python
import jax
import jax.numpy as jnp
import numpy as np
from jax import lax
from jax.experimental import pallas as pl
from jax.experimental.pallas import tpu as pltpu
from jax.sharding import Mesh
from jax.sharding import PartitionSpec as P

PAD = 48
CHUNK = 640
STRIDE = 64
SWAP = ((0, 1), (1, 0))
C0 = 0.7978845608028654
C1 = 0.044715


def hidden_kernel(scale_ref, rows_ref, grad_ref, w_in_ref, w_out_ref, dw_ref, hidden_ref, dpre_ref):
    scale_in = scale_ref[0]
    scale_out = scale_ref[1]
    rows = rows_ref[...]
    grad = grad_ref[...]
    w_in = w_in_ref[...].reshape(rows.shape[1], -1)
    w_out = w_out_ref[...].reshape(-1, grad.shape[1])
    pre = jnp.dot(rows, w_in, preferred_element_type=jnp.float32) * scale_in
    d_hidden = (
        lax.dot_general(grad, w_out, (((1,), (1,)), ((), ())), preferred_element_type=jnp.float32)
        * scale_out
    )
    square = pre * pre
    tanh = jnp.tanh(C0 * (pre + C1 * (square * pre)))
    half = 0.5 * (1.0 + tanh)
    hidden_ref[...] = (pre * half).astype(jnp.bfloat16)
    slope = half + (0.5 * C0) * pre * (1.0 - tanh * tanh) * (1.0 + (3.0 * C1) * square)
    d_pre = (slope * d_hidden).astype(jnp.bfloat16)
    dpre_ref[...] = d_pre
    dw = lax.dot_general(rows, d_pre, (((0,), (0,)), ((), ())), preferred_element_type=jnp.float32)
    dw = (dw * scale_in).astype(dw_ref.dtype)
    for z in range(dw.shape[0] // PAD):
        dw_ref[z * STRIDE : z * STRIDE + PAD] = dw[z * PAD : (z + 1) * PAD]
        dw_ref[z * STRIDE + PAD : (z + 1) * STRIDE] = jnp.zeros((STRIDE - PAD, CHUNK), dw_ref.dtype)


def hidden_of(scales, rows, grads, weights):
    count, depth = rows.shape
    width = grads.shape[1]
    zs = weights.shape[0]
    chunks = 2
    by_chunk = pl.BlockSpec((count, CHUNK), lambda r: (0, r))
    return pl.pallas_call(
        hidden_kernel,
        grid=(chunks,),
        in_specs=[
            pl.BlockSpec(memory_space=pltpu.SMEM),
            pl.BlockSpec((count, depth), lambda r: (0, 0)),
            pl.BlockSpec((count, width), lambda r: (0, 0)),
            pl.BlockSpec((zs, PAD, CHUNK), lambda r: (0, 2 + r, 0)),
            pl.BlockSpec((zs // 2, 80, width), lambda r: (r, 0, 0)),
        ],
        out_specs=[pl.BlockSpec((zs * STRIDE, CHUNK), lambda r: (0, r)), by_chunk, by_chunk],
        out_shape=[
            jax.ShapeDtypeStruct((zs * STRIDE, chunks * CHUNK), jnp.bfloat16),
            jax.ShapeDtypeStruct((count, chunks * CHUNK), jnp.bfloat16),
            jax.ShapeDtypeStruct((count, chunks * CHUNK), jnp.bfloat16),
        ],
        compiler_params=pltpu.CompilerParams(vmem_limit_bytes=56 * 1024 * 1024),
        cost_estimate=pl.CostEstimate(
            flops=6 * count * width * chunks * CHUNK,
            bytes_accessed=16 * 1024 * 1024,
            transcendentals=count * chunks * CHUNK,
        ),
    )(scales, rows, grads, weights, weights)


def rows_kernel(
    scale_ref, hidden_ref, dpre_ref, w_in_ref, w_out_ref,
    out_own_ref, drow_own_ref, out_sent_ref, drow_sent_ref, peak_ref, out_acc, drow_acc,
):
    step = pl.program_id(0)
    scale_in = scale_ref[0]
    scale_out = scale_ref[1]
    w_in = w_in_ref[...].reshape(drow_acc.shape[1], -1)
    w_out = w_out_ref[...].reshape(-1, out_acc.shape[1])
    out = jnp.dot(hidden_ref[...], w_out, preferred_element_type=jnp.float32)
    drow = lax.dot_general(
        dpre_ref[...], w_in, (((1,), (1,)), ((), ())), preferred_element_type=jnp.float32
    )
    peak_in = jnp.max(jnp.abs(w_in.astype(jnp.float32)), axis=0, keepdims=True)
    peak_out = jnp.max(jnp.abs(w_out.astype(jnp.float32)), axis=0, keepdims=True)

    @pl.when(step == 0)
    def _():
        out_acc[...] = out
        drow_acc[...] = drow
        peak_ref[:, :CHUNK] = jnp.broadcast_to(peak_in, (8, CHUNK))
        peak_ref[:, CHUNK:] = jnp.broadcast_to(peak_out, (8, CHUNK))

    @pl.when(step > 0)
    def _():
        count = out_own_ref.shape[0]
        width = out_own_ref.shape[1]
        out_sum = (out_acc[...] + out) * scale_out
        drow_sum = (drow_acc[...] + drow) * scale_in
        out_own_ref[...] = out_sum[:count]
        drow_own_ref[...] = drow_sum[:count]
        out_sent_ref[...] = out_sum[count:].astype(out_sent_ref.dtype)
        drow_sent_ref[...] = drow_sum[count:].astype(drow_sent_ref.dtype)
        peak_ref[:, :CHUNK] = jnp.maximum(peak_ref[:, :CHUNK], peak_in)
        peak_ref[:, CHUNK:] = jnp.maximum(peak_ref[:, CHUNK:], peak_out)


def rows_of(scales, hidden, dpre, weights, depth):
    count = hidden.shape[0]
    zs, _, width = weights.shape
    chunks = 2
    half = count // 2
    by_chunk = pl.BlockSpec((count, CHUNK), lambda r: (0, r))
    return pl.pallas_call(
        rows_kernel,
        grid=(chunks,),
        in_specs=[
            pl.BlockSpec(memory_space=pltpu.SMEM),
            by_chunk,
            by_chunk,
            pl.BlockSpec((zs, PAD, CHUNK), lambda r: (0, 2 + r, 0)),
            pl.BlockSpec((zs // 2, 80, width), lambda r: (r, 0, 0)),
        ],
        out_specs=[
            pl.BlockSpec((half, width), lambda r: (0, 0)),
            pl.BlockSpec((half, depth), lambda r: (0, 0)),
            pl.BlockSpec((half, width), lambda r: (0, 0)),
            pl.BlockSpec((half, depth), lambda r: (0, 0)),
            pl.BlockSpec((8, 2 * CHUNK), lambda r: (0, 0)),
        ],
        out_shape=[
            jax.ShapeDtypeStruct((half, width), jnp.float32),
            jax.ShapeDtypeStruct((half, depth), jnp.float32),
            jax.ShapeDtypeStruct((half, width), jnp.bfloat16),
            jax.ShapeDtypeStruct((half, depth), jnp.bfloat16),
            jax.ShapeDtypeStruct((8, 2 * CHUNK), jnp.float32),
        ],
        scratch_shapes=[
            pltpu.VMEM((count, width), jnp.float32),
            pltpu.VMEM((count, depth), jnp.float32),
        ],
        compiler_params=pltpu.CompilerParams(vmem_limit_bytes=56 * 1024 * 1024),
        cost_estimate=pl.CostEstimate(
            flops=4 * count * width * chunks * CHUNK,
            bytes_accessed=16 * 1024 * 1024,
            transcendentals=0,
        ),
    )(scales, hidden, dpre, weights, weights)


def placement(width, zs):
    per = width // (2 * zs)
    table = np.zeros((width, zs * PAD), np.float32)
    for half in range(2):
        for z in range(zs):
            for i in range(per):
                table[(half * zs + z) * per + i, z * PAD + half * per + i] = 1.0
    return table


def body(images, router, w_in, w_out, history, cotangent):
    bf16 = jnp.bfloat16
    f32 = jnp.float32
    width = images.shape[2]
    count = images.shape[0]
    zs = lax.axis_size("z")
    n_expert = lax.axis_size("x") * lax.axis_size("yl") * lax.axis_size("c")
    per_expert = router.shape[1] // n_expert
    along = ("x", "yl", "c")
    yh = lax.axis_index("yh")

    local = w_in[0]
    ff = local.shape[1] // 2
    stay = jnp.where(yh == 0, local[:, :ff], local[:, ff:])
    swap = jnp.where(yh == 0, local[:, ff:], local[:, :ff])
    got = lax.ppermute(swap, "yh", SWAP)
    stay = jnp.stack([stay[:, :CHUNK], stay[:, CHUNK:]])
    got = jnp.stack([got[:, :CHUNK], got[:, CHUNK:]])
    low = jnp.where(yh == 0, stay, got)
    high = jnp.where(yh == 0, got, stay)
    gap = jnp.zeros((2, PAD - 40, CHUNK), bf16)
    in_part = jnp.concatenate([low, high, gap], 1).reshape(2 * PAD, CHUNK)
    block = jnp.concatenate([w_out[0], jnp.zeros((16, CHUNK), bf16), in_part], 0)
    weights = lax.all_gather(block, "z", axis=0, tiled=False)

    scales = jnp.max(history[0], axis=1) / 448.0

    logits = jnp.einsum("bpd,ds->bps", images, router, preferred_element_type=f32)
    dispatch = jax.nn.softmax(logits, axis=1)
    combine = jax.nn.softmax(logits, axis=2)
    dispatch_b = dispatch.astype(bf16)
    combine_b = combine.astype(bf16)
    slot_in = jnp.einsum("bps,bpd->bsd", dispatch_b, images, preferred_element_type=f32).astype(bf16)
    d_slot_out = jnp.einsum("bps,bpd->bsd", combine_b, cotangent, preferred_element_type=f32).astype(bf16)
    both = jnp.stack([slot_in, d_slot_out]).reshape(2, count, n_expert, per_expert, width)
    both = both.transpose(2, 0, 1, 3, 4)
    routed = lax.all_to_all(both, along, split_axis=0, concat_axis=0, tiled=True)
    routed = routed.transpose(1, 0, 2, 3, 4).reshape(2, -1, width)
    twin = lax.ppermute(routed, "yh", SWAP)
    rows = jnp.concatenate([routed[0], twin[0]], 0)
    grads = jnp.concatenate([routed[1], twin[1]], 0)
    spread = jnp.asarray(placement(width, zs), bf16)
    rows = jnp.dot(rows, spread, preferred_element_type=f32).astype(bf16)

    dw, hidden, dpre = hidden_of(scales, rows, grads, weights)

    out_own, drow_own, out_sent, drow_sent, peaks = rows_of(scales, hidden, dpre, weights, rows.shape[1])
    fetched = lax.ppermute(jnp.concatenate([out_sent, drow_sent], 1), "yh", SWAP)
    rows_out = (out_own + fetched[:, :width].astype(f32)).astype(bf16)
    d_rows = (drow_own + fetched[:, width:].astype(f32)).astype(bf16)
    d_rows = lax.dot_general(
        d_rows, spread, (((1,), (1,)), ((), ())), preferred_element_type=f32
    ).astype(bf16)
    back = jnp.stack(
        [rows_out.reshape(n_expert, -1, width), d_rows.reshape(n_expert, -1, width)], 1
    ).reshape(n_expert, 2, count, per_expert, width)
    returned = lax.all_to_all(back, along, split_axis=0, concat_axis=0, tiled=True)
    returned = returned.transpose(1, 2, 0, 3, 4).reshape(2, count, -1, width)

    part = lax.psum_scatter(dw, "z", scatter_dimension=0, tiled=True)
    keep = jnp.where(yh == 0, part[:20], part[20:40])
    give = jnp.where(yh == 0, part[20:40], part[:20])
    peaks = peaks[:1].astype(bf16)
    got = lax.ppermute(jnp.concatenate([give, peaks], 0), "yh", SWAP)
    theirs = got[:20]
    d_w_in = jnp.concatenate(
        [jnp.where(yh == 0, keep, theirs), jnp.where(yh == 0, theirs, keep)], 1
    )[None]
    peaks = jnp.maximum(peaks[0], got[20]).reshape(2, -1).astype(f32)
    peaks = jnp.max(peaks, axis=1, keepdims=True)
    new_history = jnp.concatenate([peaks, history[0, :, :-1]], axis=1)[None]

    slot_out = returned[0]
    d_slot_in = returned[1]
    output = jnp.einsum("bps,bsd->bpd", combine_b, slot_out, preferred_element_type=f32).astype(bf16)
    d_combine = jnp.einsum("bpd,bsd->bps", cotangent, slot_out, preferred_element_type=f32)
    d_dispatch = jnp.einsum("bpd,bsd->bps", images, d_slot_in, preferred_element_type=f32)
    d_logits = dispatch * (d_dispatch - jnp.sum(dispatch * d_dispatch, axis=1, keepdims=True))
    d_logits = d_logits + combine * (d_combine - jnp.sum(combine * d_combine, axis=2, keepdims=True))
    d_logits = d_logits.astype(bf16)
    d_images = jnp.einsum("bps,bsd->bpd", dispatch_b, d_slot_in, preferred_element_type=f32)
    d_images = d_images + jnp.einsum("bps,ds->bpd", d_logits, router, preferred_element_type=f32)
    d_images = d_images.astype(bf16)
    return (output, d_images, d_w_in, new_history)


def solution(mesh):
    fine = Mesh(mesh.devices.reshape(2, 16, 4, 2, 2), ("yh", "z", "x", "yl", "c"))
    dp = ("yh", "z")
    expert = ("x", "yl", "c")
    every = dp + expert
    return jax.shard_map(
        body,
        mesh=fine,
        in_specs=(
            P(every, None, None),
            P(),
            P(expert, dp, None),
            P(expert, dp, None),
            P(expert, None, None),
            P(every, None, None),
        ),
        out_specs=(
            P(every, None, None),
            P(every, None, None),
            P(expert, dp, None),
            P(expert, None, None),
        ),
        check_vma=False,
    )
```

```python
import jax
import jax.numpy as jnp
import numpy as np
from jax import lax
from jax.experimental import pallas as pl
from jax.experimental.pallas import tpu as pltpu
from jax.sharding import Mesh
from jax.sharding import PartitionSpec as P

PAD = 48
CHUNK = 640
STRIDE = 64
SWAP = ((0, 1), (1, 0))
C0 = 0.7978845608028654
C1 = 0.044715


def hidden_kernel(
    scale_ref, rows_ref, turned_ref, grad_ref, w_in_ref, w_out_ref, dw_ref, hidden_ref, dpre_ref
):
    scale_in = scale_ref[0]
    scale_out = scale_ref[1]
    rows = rows_ref[...]
    grad = grad_ref[...]
    w_in = w_in_ref[...].reshape(rows.shape[1], -1)
    w_out = w_out_ref[...].reshape(-1, grad.shape[1])
    pre = jnp.dot(rows, w_in, preferred_element_type=jnp.float32) * scale_in
    d_hidden = (
        lax.dot_general(grad, w_out, (((1,), (1,)), ((), ())), preferred_element_type=jnp.float32)
        * scale_out
    )
    square = pre * pre
    tanh = jnp.tanh(C0 * (pre + C1 * (square * pre)))
    half = 0.5 * (1.0 + tanh)
    hidden_ref[...] = (pre * half).astype(jnp.bfloat16)
    slope = half + (0.5 * C0) * pre * (1.0 - tanh * tanh) * (1.0 + (3.0 * C1) * square)
    d_pre = (slope * d_hidden).astype(jnp.bfloat16)
    dpre_ref[...] = d_pre
    dw = jnp.dot(turned_ref[...], d_pre, preferred_element_type=jnp.float32)
    dw = (dw * scale_in).astype(dw_ref.dtype)
    for z in range(dw.shape[0] // PAD):
        dw_ref[z * STRIDE : z * STRIDE + PAD] = dw[z * PAD : (z + 1) * PAD]
        dw_ref[z * STRIDE + PAD : (z + 1) * STRIDE] = jnp.zeros((STRIDE - PAD, CHUNK), dw_ref.dtype)


def hidden_of(scales, rows, turned, grads, weights):
    count, depth = rows.shape
    width = grads.shape[1]
    zs = weights.shape[0]
    chunks = 2
    by_chunk = pl.BlockSpec((count, CHUNK), lambda r: (0, r))
    return pl.pallas_call(
        hidden_kernel,
        grid=(chunks,),
        in_specs=[
            pl.BlockSpec(memory_space=pltpu.SMEM),
            pl.BlockSpec((count, depth), lambda r: (0, 0)),
            pl.BlockSpec((depth, count), lambda r: (0, 0)),
            pl.BlockSpec((count, width), lambda r: (0, 0)),
            pl.BlockSpec((zs, PAD, CHUNK), lambda r: (0, 2 + r, 0)),
            pl.BlockSpec((zs // 2, 80, width), lambda r: (r, 0, 0)),
        ],
        out_specs=[pl.BlockSpec((zs * STRIDE, CHUNK), lambda r: (0, r)), by_chunk, by_chunk],
        out_shape=[
            jax.ShapeDtypeStruct((zs * STRIDE, chunks * CHUNK), jnp.bfloat16),
            jax.ShapeDtypeStruct((count, chunks * CHUNK), jnp.bfloat16),
            jax.ShapeDtypeStruct((count, chunks * CHUNK), jnp.bfloat16),
        ],
        compiler_params=pltpu.CompilerParams(vmem_limit_bytes=56 * 1024 * 1024),
        cost_estimate=pl.CostEstimate(
            flops=6 * count * width * chunks * CHUNK,
            bytes_accessed=16 * 1024 * 1024,
            transcendentals=count * chunks * CHUNK,
        ),
    )(scales, rows, turned, grads, weights, weights)


def rows_kernel(
    scale_ref, hidden_ref, dpre_ref, w_in_ref, w_out_ref,
    out_own_ref, drow_own_ref, out_sent_ref, drow_sent_ref, peak_ref, out_acc, drow_acc,
):
    step = pl.program_id(0)
    scale_in = scale_ref[0]
    scale_out = scale_ref[1]
    w_in = w_in_ref[...].reshape(drow_acc.shape[1], -1)
    w_out = w_out_ref[...].reshape(-1, out_acc.shape[1])
    out = jnp.dot(hidden_ref[...], w_out, preferred_element_type=jnp.float32)
    drow = lax.dot_general(
        dpre_ref[...], w_in, (((1,), (1,)), ((), ())), preferred_element_type=jnp.float32
    )
    peak_in = jnp.max(jnp.abs(w_in.astype(jnp.float32)), axis=0, keepdims=True)
    peak_out = jnp.max(jnp.abs(w_out.astype(jnp.float32)), axis=0, keepdims=True)

    @pl.when(step == 0)
    def _():
        out_acc[...] = out
        drow_acc[...] = drow
        peak_ref[:, :CHUNK] = jnp.broadcast_to(peak_in, (8, CHUNK))
        peak_ref[:, CHUNK:] = jnp.broadcast_to(peak_out, (8, CHUNK))

    @pl.when(step > 0)
    def _():
        count = out_own_ref.shape[0]
        width = out_own_ref.shape[1]
        out_sum = (out_acc[...] + out) * scale_out
        drow_sum = (drow_acc[...] + drow) * scale_in
        out_own_ref[...] = out_sum[:count]
        drow_own_ref[...] = drow_sum[:count]
        out_sent_ref[...] = out_sum[count:].astype(out_sent_ref.dtype)
        drow_sent_ref[...] = drow_sum[count:].astype(drow_sent_ref.dtype)
        peak_ref[:, :CHUNK] = jnp.maximum(peak_ref[:, :CHUNK], peak_in)
        peak_ref[:, CHUNK:] = jnp.maximum(peak_ref[:, CHUNK:], peak_out)


def rows_of(scales, hidden, dpre, weights, depth):
    count = hidden.shape[0]
    zs, _, width = weights.shape
    chunks = 2
    half = count // 2
    by_chunk = pl.BlockSpec((count, CHUNK), lambda r: (0, r))
    return pl.pallas_call(
        rows_kernel,
        grid=(chunks,),
        in_specs=[
            pl.BlockSpec(memory_space=pltpu.SMEM),
            by_chunk,
            by_chunk,
            pl.BlockSpec((zs, PAD, CHUNK), lambda r: (0, 2 + r, 0)),
            pl.BlockSpec((zs // 2, 80, width), lambda r: (r, 0, 0)),
        ],
        out_specs=[
            pl.BlockSpec((half, width), lambda r: (0, 0)),
            pl.BlockSpec((half, depth), lambda r: (0, 0)),
            pl.BlockSpec((half, width), lambda r: (0, 0)),
            pl.BlockSpec((half, depth), lambda r: (0, 0)),
            pl.BlockSpec((8, 2 * CHUNK), lambda r: (0, 0)),
        ],
        out_shape=[
            jax.ShapeDtypeStruct((half, width), jnp.float32),
            jax.ShapeDtypeStruct((half, depth), jnp.float32),
            jax.ShapeDtypeStruct((half, width), jnp.bfloat16),
            jax.ShapeDtypeStruct((half, depth), jnp.bfloat16),
            jax.ShapeDtypeStruct((8, 2 * CHUNK), jnp.float32),
        ],
        scratch_shapes=[
            pltpu.VMEM((count, width), jnp.float32),
            pltpu.VMEM((count, depth), jnp.float32),
        ],
        compiler_params=pltpu.CompilerParams(vmem_limit_bytes=56 * 1024 * 1024),
        cost_estimate=pl.CostEstimate(
            flops=4 * count * width * chunks * CHUNK,
            bytes_accessed=16 * 1024 * 1024,
            transcendentals=0,
        ),
    )(scales, hidden, dpre, weights, weights)


def placement(width, zs):
    per = width // (2 * zs)
    table = np.zeros((width, zs * PAD), np.float32)
    for half in range(2):
        for z in range(zs):
            for i in range(per):
                table[(half * zs + z) * per + i, z * PAD + half * per + i] = 1.0
    return table


def body(images, router, w_in, w_out, history, cotangent):
    bf16 = jnp.bfloat16
    f32 = jnp.float32
    width = images.shape[2]
    count = images.shape[0]
    zs = lax.axis_size("z")
    n_expert = lax.axis_size("x") * lax.axis_size("yl") * lax.axis_size("c")
    per_expert = router.shape[1] // n_expert
    along = ("x", "yl", "c")
    yh = lax.axis_index("yh")

    local = w_in[0]
    ff = local.shape[1] // 2
    stay = jnp.where(yh == 0, local[:, :ff], local[:, ff:])
    swap = jnp.where(yh == 0, local[:, ff:], local[:, :ff])
    got = lax.ppermute(swap, "yh", SWAP)
    stay = jnp.stack([stay[:, :CHUNK], stay[:, CHUNK:]])
    got = jnp.stack([got[:, :CHUNK], got[:, CHUNK:]])
    low = jnp.where(yh == 0, stay, got)
    high = jnp.where(yh == 0, got, stay)
    gap = jnp.zeros((2, PAD - 40, CHUNK), bf16)
    in_part = jnp.concatenate([low, high, gap], 1).reshape(2 * PAD, CHUNK)
    block = jnp.concatenate([w_out[0], jnp.zeros((16, CHUNK), bf16), in_part], 0)
    weights = lax.all_gather(block, "z", axis=0, tiled=False)

    scales = jnp.max(history[0], axis=1) / 448.0

    logits = jnp.einsum("bpd,ds->bps", images, router, preferred_element_type=f32)
    dispatch = jax.nn.softmax(logits, axis=1)
    combine = jax.nn.softmax(logits, axis=2)
    dispatch_b = dispatch.astype(bf16)
    combine_b = combine.astype(bf16)
    slot_in = jnp.einsum("bps,bpd->bsd", dispatch_b, images, preferred_element_type=f32).astype(bf16)
    d_slot_out = jnp.einsum("bps,bpd->bsd", combine_b, cotangent, preferred_element_type=f32).astype(bf16)
    both = jnp.stack([slot_in, d_slot_out]).reshape(2, count, n_expert, per_expert, width)
    both = both.transpose(2, 0, 1, 3, 4)
    routed = lax.all_to_all(both, along, split_axis=0, concat_axis=0, tiled=True)
    routed = routed.transpose(1, 0, 2, 3, 4).reshape(2, -1, width)
    twin = lax.ppermute(routed, "yh", SWAP)
    rows = jnp.concatenate([routed[0], twin[0]], 0)
    grads = jnp.concatenate([routed[1], twin[1]], 0)
    spread = jnp.asarray(placement(width, zs), bf16)
    turned = lax.dot_general(
        spread, rows, (((0,), (1,)), ((), ())), preferred_element_type=f32
    ).astype(bf16)
    rows = jnp.dot(rows, spread, preferred_element_type=f32).astype(bf16)

    dw, hidden, dpre = hidden_of(scales, rows, turned, grads, weights)

    out_own, drow_own, out_sent, drow_sent, peaks = rows_of(scales, hidden, dpre, weights, rows.shape[1])
    fetched = lax.ppermute(jnp.concatenate([out_sent, drow_sent], 1), "yh", SWAP)
    rows_out = (out_own + fetched[:, :width].astype(f32)).astype(bf16)
    d_rows = (drow_own + fetched[:, width:].astype(f32)).astype(bf16)
    d_rows = lax.dot_general(
        d_rows, spread, (((1,), (1,)), ((), ())), preferred_element_type=f32
    ).astype(bf16)
    back = jnp.stack(
        [rows_out.reshape(n_expert, -1, width), d_rows.reshape(n_expert, -1, width)], 1
    ).reshape(n_expert, 2, count, per_expert, width)
    returned = lax.all_to_all(back, along, split_axis=0, concat_axis=0, tiled=True)
    returned = returned.transpose(1, 2, 0, 3, 4).reshape(2, count, -1, width)

    part = lax.psum_scatter(dw, "z", scatter_dimension=0, tiled=True)
    keep = jnp.where(yh == 0, part[:20], part[20:40])
    give = jnp.where(yh == 0, part[20:40], part[:20])
    peaks = peaks[:1].astype(bf16)
    got = lax.ppermute(jnp.concatenate([give, peaks], 0), "yh", SWAP)
    theirs = got[:20]
    d_w_in = jnp.concatenate(
        [jnp.where(yh == 0, keep, theirs), jnp.where(yh == 0, theirs, keep)], 1
    )[None]
    peaks = jnp.maximum(peaks[0], got[20]).reshape(2, -1).astype(f32)
    peaks = jnp.max(peaks, axis=1, keepdims=True)
    new_history = jnp.concatenate([peaks, history[0, :, :-1]], axis=1)[None]

    slot_out = returned[0]
    d_slot_in = returned[1]
    output = jnp.einsum("bps,bsd->bpd", combine_b, slot_out, preferred_element_type=f32).astype(bf16)
    d_combine = jnp.einsum("bpd,bsd->bps", cotangent, slot_out, preferred_element_type=f32)
    d_dispatch = jnp.einsum("bpd,bsd->bps", images, d_slot_in, preferred_element_type=f32)
    d_logits = dispatch * (d_dispatch - jnp.sum(dispatch * d_dispatch, axis=1, keepdims=True))
    d_logits = d_logits + combine * (d_combine - jnp.sum(combine * d_combine, axis=2, keepdims=True))
    d_logits = d_logits.astype(bf16)
    d_images = jnp.einsum("bps,bsd->bpd", dispatch_b, d_slot_in, preferred_element_type=f32)
    d_images = d_images + jnp.einsum("bps,ds->bpd", d_logits, router, preferred_element_type=f32)
    d_images = d_images.astype(bf16)
    return (output, d_images, d_w_in, new_history)


def solution(mesh):
    fine = Mesh(mesh.devices.reshape(2, 16, 4, 2, 2), ("yh", "z", "x", "yl", "c"))
    dp = ("yh", "z")
    expert = ("x", "yl", "c")
    every = dp + expert
    return jax.shard_map(
        body,
        mesh=fine,
        in_specs=(
            P(every, None, None),
            P(),
            P(expert, dp, None),
            P(expert, dp, None),
            P(expert, None, None),
            P(every, None, None),
        ),
        out_specs=(
            P(every, None, None),
            P(every, None, None),
            P(expert, dp, None),
            P(expert, None, None),
        ),
        check_vma=False,
    )
```
